1024 devices in a mesh: row: 32 (over z, x_hi, core), col: 32 (over y, x_lo).
Axes of the slice: x: 8 (x_hi: 2, x_lo: 4; x = x_hi * 4 + x_lo), y: 8, z: 8, core: 2. Of those that a mesh axis runs over, the one named last changes fastest.
Arguments:
- occ_irrep: int32 [128], replicated, may hold values from 0 to 7
- vir_irrep: int32 [1024], replicated, may hold values from 0 to 7
- w_slab: bfloat16 [12288, 131072], P('row', 'col'), may hold values from -0.046875 to 0.046875
- amplitudes: bfloat16 [256, 131072], P('row', 'col'), may hold values from -6 to 6
Outputs:
- cycle_term: float32 [256, 12288], P('col', 'row')
The draws below stay inside these ranges and needn't reach their ends.
Inputs may be any that keep to these rules, and one draw needn't show every extreme that they name: `occ_irrep`: D2h irrep labels. `vir_irrep`: D2h irrep labels.
All inputs are finite; a program needn't handle non-finite values.
Results may differ from the reference program's by a relative error of at most 0.0003.
Values may be sent and summed in bfloat16 or wider, within the bound.
No kernel may reach another device: no remote copies, remote signals or barrier semaphores. Data moves between devices by JAX's collectives and lax.ppermute only.
A program may use at most 32 MiB of HBM per device.

```python
import jax
import jax.numpy as jnp
from jax import lax

NOCC = 128
NVIR = 1024
NCOL = 256
KORD = 131072
ROWS = 12288
N_COL = 32


def touch_ends(drawn, own_key, smallest, high):
    longest = drawn.shape.index(max(drawn.shape))
    spots = []
    for shift in (0, 1):
        where = [jax.random.randint(jax.random.fold_in(own_key, axis), (), 0, length) for axis, length in enumerate(drawn.shape)]
        where[longest] = (where[longest] + shift) % drawn.shape[longest]
        spots.append(tuple(where))
    return drawn.at[spots[0]].set(smallest).at[spots[1]].set(high)


def raised(entries, key, source, target, parts, factor):
    owner, partner = [(jnp.arange(entries.shape[dim]) // (entries.shape[dim] // parts)).reshape([-1 if axis == dim else 1 for axis in range(entries.ndim)]) for dim in (source, target)]
    chosen = jax.random.permutation(key, parts)[partner]
    strong = (owner == chosen) | (owner == (partner + parts // 2) % parts)
    return jnp.where(strong, factor * entries, entries)


def steps_of(own_key, dims, cuts, smallest, top_value):
    level, own = 1.0, jax.random.fold_in(own_key, 6)
    for dim, shards_of in cuts:
        steps = jnp.exp(jax.random.uniform(jax.random.fold_in(own, dim), (shards_of,), jnp.float32, smallest / len(cuts), top_value / len(cuts)))
        level = level * jnp.repeat(steps, dims[dim] // shards_of).reshape([-1 if axis == dim else 1 for axis in range(len(dims))])
    return level


def normal_values(rng, extent, spread, reach, shards=(), kind=jnp.bfloat16):
    factor_of = steps_of(rng, extent, shards, -0.22, 0.18) if shards else 1.0
    array = jax.random.normal(rng, extent, jnp.float32) * spread * factor_of
    return jnp.minimum(jnp.maximum(array, -reach), reach).astype(kind)


def heavy_noise(stream_key, extent, spread, limit, cuts, heavy, kind=jnp.bfloat16):
    values = spread * jax.random.normal(stream_key, extent, jnp.float32)
    if cuts:
        values = values * steps_of(stream_key, extent, cuts, -0.22, 0.18)
    return jnp.clip(raised(values, jax.random.fold_in(stream_key, 3), *heavy), -limit, limit).astype(kind)


def setup_inputs(seed: int = 0) -> dict:
    streams_of = jax.random.split(jax.random.key(seed), 5)
    occ_irrep = touch_ends(jax.random.randint(streams_of[0], (NOCC,), 0, 8), jax.random.fold_in(streams_of[0], 1), 0, 7).astype(jnp.int32)
    vir_irrep = touch_ends(jax.random.randint(streams_of[1], (NVIR,), 0, 8), jax.random.fold_in(streams_of[1], 1), 0, 7).astype(jnp.int32)
    w_slab = normal_values(streams_of[2], (ROWS, KORD), (KORD // 8) ** -0.5, 0.046875, ((0, 32), (1, 32)))
    amplitudes = heavy_noise(streams_of[3], (NCOL, KORD), 1.0, 6.0, ((0, 32), (1, 32)), (1, 0, 32, 2.75))
    return {"occ_irrep": occ_irrep, "vir_irrep": vir_irrep, "w_slab": w_slab, "amplitudes": amplitudes}


def labels(index, occ_irrep, vir_irrep):
    nvir = vir_irrep.shape[0]
    occ_part = jnp.take(occ_irrep, index // nvir)
    vir_part = jnp.take(vir_irrep, index % nvir)
    return jnp.bitwise_xor(occ_part, vir_part)


def reference(occ_irrep, vir_irrep, w_slab, amplitudes):
    nrows = w_slab.shape[0]
    korder = w_slab.shape[1]
    ncols = amplitudes.shape[0]
    block = korder // N_COL
    row_labels = labels(jnp.arange(nrows, dtype=jnp.int32), occ_irrep, vir_irrep)

    def accumulate(total, step):
        start = (step * block).astype(jnp.int32)
        w_block = lax.dynamic_slice_in_dim(w_slab, start, block, 1)
        a_block = lax.dynamic_slice_in_dim(amplitudes, start, block, 1)
        col_labels = labels(start + jnp.arange(block, dtype=jnp.int32), occ_irrep, vir_irrep)
        keep = row_labels[:, None] == col_labels[None, :]
        masked = jnp.where(keep, w_block, jnp.zeros_like(w_block))
        total = total + jnp.dot(a_block, masked.T, preferred_element_type=jnp.float32)
        return total, None

    start_total = jnp.zeros((ncols, nrows), jnp.float32)
    result, _ = lax.scan(accumulate, start_total, jnp.arange(N_COL, dtype=jnp.int32))
    return result
```

```python
import jax
import jax.numpy as jnp
from jax import lax
from jax.sharding import PartitionSpec as P


def spans(start, length, occ_irrep, vir_irrep):
    nvir = vir_irrep.shape[0]
    first, offset = start // nvir, start % nvir
    count = -(-length // nvir)
    vir = lax.dynamic_slice_in_dim(jnp.tile(vir_irrep, count + 1), offset, length, 0)
    position = offset + jnp.arange(length, dtype=jnp.int32)
    occ = jnp.zeros((length,), jnp.int32)
    for step in range(count + 1):
        label = lax.dynamic_index_in_dim(occ_irrep, jnp.minimum(first + step, occ_irrep.shape[0] - 1), 0, False)
        occ = jnp.where(position // nvir == step, label, occ)
    return jnp.bitwise_xor(occ, vir)


def body(occ_irrep, vir_irrep, w_slab, amplitudes):
    nrows, width = w_slab.shape
    here, depth = amplitudes.shape[0], amplitudes.shape[1]
    n_row, n_col = lax.axis_size("row"), lax.axis_size("col")
    row_labels = spans(lax.axis_index("row") * nrows, nrows, occ_irrep, vir_irrep)
    col_labels = spans(lax.axis_index("col") * width, width, occ_irrep, vir_irrep)
    keep = row_labels[:, None] == col_labels[None, :]
    masked = jnp.where(keep, w_slab, jnp.zeros_like(w_slab))

    chips = n_row // 2
    groups = [[2 * chip + core for chip in range(chips)] for core in range(2)]
    copies = jnp.broadcast_to(amplitudes[None], (chips, here, depth))
    own = lax.all_to_all(copies, "row", 0, 0, axis_index_groups=groups).reshape(chips * here, depth)
    other = lax.ppermute(own, "row", [(i, i ^ 1) for i in range(n_row)])

    dims = (((1,), (1,)), ((), ()))
    mine = lax.dot_general(own, masked, dims, preferred_element_type=jnp.float32)
    theirs = lax.dot_general(other, masked, dims, preferred_element_type=jnp.float32)
    is_first = lax.axis_index("row") % 2 == 0
    low, high = jnp.where(is_first, mine, theirs), jnp.where(is_first, theirs, mine)
    parts = jnp.stack([low.reshape(chips, here, nrows), high.reshape(chips, here, nrows)], 1)
    sent = lax.all_to_all(parts.reshape(n_col, here, nrows), "col", 0, 0)
    return sent.sum(0)


def solution(mesh):
    placed = (P(), P(), P("row", "col"), P("row", "col"))
    return jax.shard_map(
        body, mesh=mesh, in_specs=placed, out_specs=P("col", "row"), check_vma=False
    )
```

```python
import jax
import jax.numpy as jnp
from jax import lax
from jax.experimental import pallas as pl
from jax.experimental.pallas import tpu as pltpu
from jax.sharding import PartitionSpec as P

BAND = 128


def against(left, w):
    return lax.dot_general(left, w, (((1,), (1,)), ((), ())), preferred_element_type=jnp.float32)


def band_labels(start, band, occ_ref, vir):
    nocc, nvir = occ_ref.shape[0], vir.shape[1]
    row = start + lax.broadcasted_iota(jnp.int32, (band, 1), 0)
    chosen = lax.broadcasted_iota(jnp.int32, (band, nvir), 1) == row % nvir
    vir_part = jnp.sum(jnp.where(chosen, jnp.broadcast_to(vir, (band, nvir)), 0), axis=1, keepdims=True)
    first = start // nvir
    following = occ_ref[jnp.minimum(first + 1, nocc - 1)]
    return vir_part ^ jnp.where(row // nvir == first, occ_ref[first], following)


def mask_kernel(place_ref, occ_ref, vir_ref, *refs):
    *own_refs, w_ref, masked_ref, mine_ref, sems = refs
    nrows, width = masked_ref.shape
    nvir = vir_ref.shape[1]
    vir = vir_ref[...]
    spans = [pl.ds(start, BAND) for start in range(0, nrows, BAND)]
    copies = [pltpu.make_async_copy(w_ref.at[span], masked_ref.at[span], sems.at[i]) for i, span in enumerate(spans)]
    for copy in copies:
        copy.start()
    col_labels = [vir ^ occ_ref[place_ref[1] // nvir + part] for part in range(width // nvir)]
    for i, (span, copy) in enumerate(zip(spans, copies)):
        row_labels = band_labels(place_ref[0] + i * BAND, BAND, occ_ref, vir)
        copy.wait()
        for part, labels in enumerate(col_labels):
            cols = pl.ds(part * nvir, nvir)
            w = masked_ref[span, cols]
            masked_ref[span, cols] = jnp.where(row_labels == labels, w, jnp.zeros_like(w))
        for s, own_ref in enumerate(own_refs):
            product = against(own_ref[...], masked_ref[span, :])
            mine_ref[s, :, :, span] = product.reshape(mine_ref.shape[1], mine_ref.shape[2], BAND)


def mask_and_multiply(occ_irrep, vir_irrep, w_slab, own, here):
    nrows, width = w_slab.shape
    nvir = vir_irrep.shape[0]
    rows = own[0].shape[0]
    place = jnp.stack([lax.axis_index("row") * nrows, lax.axis_index("col") * width]).astype(jnp.int32)
    smem, vmem = pl.BlockSpec(memory_space=pltpu.SMEM), pl.BlockSpec(memory_space=pltpu.VMEM)
    return pl.pallas_call(
        mask_kernel,
        in_specs=[smem, smem, vmem] + [vmem] * len(own) + [pl.BlockSpec(memory_space=pltpu.HBM)],
        out_specs=[vmem, vmem],
        out_shape=[
            jax.ShapeDtypeStruct(w_slab.shape, w_slab.dtype),
            jax.ShapeDtypeStruct((len(own), rows // here, here, nrows), jnp.float32),
        ],
        scratch_shapes=[pltpu.SemaphoreType.DMA((nrows // BAND,))],
        compiler_params=pltpu.CompilerParams(vmem_limit_bytes=48 * 1024 * 1024),
        cost_estimate=pl.CostEstimate(
            flops=2 * len(own) * rows * width * nrows, bytes_accessed=4 * nrows * width, transcendentals=0
        ),
    )(place, occ_irrep, vir_irrep.reshape(1, nvir), *own, w_slab)


def place_kernel(me_ref, other_ref, w_ref, mine_ref, out_ref):
    me = me_ref[0]
    core, side = me % 2, me // 2 % 2
    count, chips, here, nrows = mine_ref.shape
    product = against(other_ref[...], w_ref[...]).reshape(mine_ref.shape)
    for s in range(count):
        if count == 1:
            out_ref[:, pl.ds(core, 1)] = mine_ref[s][:, None]
            out_ref[:, pl.ds(1 - core, 1)] = product[s][:, None]
        else:
            out_ref[:, pl.ds(side ^ s, 1), pl.ds(core, 1)] = mine_ref[s][:, None, None]
            out_ref[:, pl.ds(side ^ s, 1), pl.ds(1 - core, 1)] = product[s][:, None, None]


def multiply_and_place(other, masked, mine):
    nrows, width = masked.shape
    count, chips, here, _ = mine.shape
    shape = (chips, 2, here, nrows) if count == 1 else (chips, count, 2, here, nrows)
    me = lax.axis_index("row").astype(jnp.int32).reshape(1)
    vmem = pl.BlockSpec(memory_space=pltpu.VMEM)
    return pl.pallas_call(
        place_kernel,
        in_specs=[pl.BlockSpec(memory_space=pltpu.SMEM), vmem, vmem, vmem],
        out_specs=vmem,
        out_shape=jax.ShapeDtypeStruct(shape, jnp.float32),
        compiler_params=pltpu.CompilerParams(vmem_limit_bytes=8 * 1024 * 1024),
        cost_estimate=pl.CostEstimate(
            flops=2 * other.shape[0] * width * nrows, bytes_accessed=2 * nrows * width, transcendentals=0
        ),
    )(me, other, masked, mine)


def body(occ_irrep, vir_irrep, w_slab, amplitudes):
    nrows, width = w_slab.shape
    here = amplitudes.shape[0]
    n_row = lax.axis_size("row")
    chips = n_row // 2
    cores = [[2 * chip + core for chip in range(chips)] for core in range(2)]
    copies = jnp.broadcast_to(amplitudes[None], (chips, here, width))
    own = lax.all_to_all(copies, "row", 0, 0, axis_index_groups=cores).reshape(chips * here, width)
    other = lax.ppermute(own, "row", [(i, i ^ 1) for i in range(n_row)])
    masked, mine = mask_and_multiply(occ_irrep, vir_irrep, w_slab, [own], here)
    parts = multiply_and_place(other, masked, mine)
    sent = lax.all_to_all(parts.reshape(n_row, here, nrows), "col", 0, 0)
    return sent.sum(0)


def solution(mesh):
    placed = (P(), P(), P("row", "col"), P("row", "col"))
    return jax.shard_map(
        body, mesh=mesh, in_specs=placed, out_specs=P("col", "row"), check_vma=False
    )
```

```python
import jax
import jax.numpy as jnp
from jax import lax
from jax.experimental import pallas as pl
from jax.experimental.pallas import tpu as pltpu
from jax.sharding import PartitionSpec as P

BAND = 128


def against(left, w):
    return lax.dot_general(left, w, (((1,), (1,)), ((), ())), preferred_element_type=jnp.float32)


def band_labels(start, band, occ_ref, vir):
    nocc, nvir = occ_ref.shape[0], vir.shape[1]
    row = start + lax.broadcasted_iota(jnp.int32, (band, 1), 0)
    chosen = lax.broadcasted_iota(jnp.int32, (band, nvir), 1) == row % nvir
    vir_part = jnp.sum(jnp.where(chosen, jnp.broadcast_to(vir, (band, nvir)), 0), axis=1, keepdims=True)
    first = start // nvir
    following = occ_ref[jnp.minimum(first + 1, nocc - 1)]
    return vir_part ^ jnp.where(row // nvir == first, occ_ref[first], following)


def mask_kernel(place_ref, occ_ref, vir_ref, *refs):
    *own_refs, w_ref, masked_ref, mine_ref, sems = refs
    nrows, width = masked_ref.shape
    nvir = vir_ref.shape[1]
    vir = vir_ref[...]
    spans = [pl.ds(start, BAND) for start in range(0, nrows, BAND)]
    copies = [pltpu.make_async_copy(w_ref.at[span], masked_ref.at[span], sems.at[i]) for i, span in enumerate(spans)]
    for copy in copies:
        copy.start()
    col_labels = [vir ^ occ_ref[place_ref[1] // nvir + part] for part in range(width // nvir)]

    def mask(i):
        row_labels = band_labels(place_ref[0] + i * BAND, BAND, occ_ref, vir)
        copies[i].wait()
        for part, labels in enumerate(col_labels):
            cols = pl.ds(part * nvir, nvir)
            w = masked_ref[spans[i], cols]
            masked_ref[spans[i], cols] = jnp.where(row_labels == labels, w, jnp.zeros_like(w))

    def multiply(i):
        for s, own_ref in enumerate(own_refs):
            product = against(own_ref[...], masked_ref[spans[i], :])
            mine_ref[s, :, :, spans[i]] = product.reshape(mine_ref.shape[1], mine_ref.shape[2], BAND)

    for i in range(len(spans)):
        mask(i)
        if i:
            multiply(i - 1)
    multiply(len(spans) - 1)


def mask_and_multiply(occ_irrep, vir_irrep, w_slab, own, here):
    nrows, width = w_slab.shape
    nvir = vir_irrep.shape[0]
    rows = own[0].shape[0]
    place = jnp.stack([lax.axis_index("row") * nrows, lax.axis_index("col") * width]).astype(jnp.int32)
    smem, vmem = pl.BlockSpec(memory_space=pltpu.SMEM), pl.BlockSpec(memory_space=pltpu.VMEM)
    return pl.pallas_call(
        mask_kernel,
        in_specs=[smem, smem, vmem] + [vmem] * len(own) + [pl.BlockSpec(memory_space=pltpu.HBM)],
        out_specs=[vmem, vmem],
        out_shape=[
            jax.ShapeDtypeStruct(w_slab.shape, w_slab.dtype),
            jax.ShapeDtypeStruct((len(own), rows // here, here, nrows), jnp.float32),
        ],
        scratch_shapes=[pltpu.SemaphoreType.DMA((nrows // BAND,))],
        compiler_params=pltpu.CompilerParams(vmem_limit_bytes=48 * 1024 * 1024),
        cost_estimate=pl.CostEstimate(
            flops=2 * len(own) * rows * width * nrows, bytes_accessed=4 * nrows * width, transcendentals=0
        ),
    )(place, occ_irrep, vir_irrep.reshape(1, nvir), *own, w_slab)


def place_kernel(me_ref, other_ref, w_ref, mine_ref, out_ref):
    core = me_ref[0] % 2
    planes = out_ref.shape[0]
    product = against(other_ref[...], w_ref[...]).reshape(mine_ref.shape)
    for value, at in ((mine_ref, core), (product, 1 - core)):
        for side in range(2):
            blocks = value[0, side * planes : (side + 1) * planes]
            out_ref[:, side, pl.ds(at, 1)] = blocks[:, None]


def multiply_and_place(other, masked, mine):
    nrows, width = masked.shape
    _, chips, here, _ = mine.shape
    shape = (chips // 2, 2, 2, here, nrows)
    me = lax.axis_index("row").astype(jnp.int32).reshape(1)
    vmem = pl.BlockSpec(memory_space=pltpu.VMEM)
    return pl.pallas_call(
        place_kernel,
        in_specs=[pl.BlockSpec(memory_space=pltpu.SMEM), vmem, vmem, vmem],
        out_specs=vmem,
        out_shape=jax.ShapeDtypeStruct(shape, jnp.float32),
        compiler_params=pltpu.CompilerParams(vmem_limit_bytes=8 * 1024 * 1024),
        cost_estimate=pl.CostEstimate(
            flops=2 * other.shape[0] * width * nrows, bytes_accessed=2 * nrows * width, transcendentals=0
        ),
    )(me, other, masked, mine)


def body(occ_irrep, vir_irrep, w_slab, amplitudes):
    nrows, width = w_slab.shape
    here = amplitudes.shape[0]
    n_row = lax.axis_size("row")
    chips = n_row // 2
    cores = [[4 * p + 2 * side + core for side in range(2) for p in range(chips // 2)] for core in range(2)]
    copies = jnp.broadcast_to(amplitudes[None], (chips, here, width))
    own = lax.all_to_all(copies, "row", 0, 0, axis_index_groups=cores).reshape(chips * here, width)
    other = lax.ppermute(own, "row", [(i, i ^ 1) for i in range(n_row)])
    masked, mine = mask_and_multiply(occ_irrep, vir_irrep, w_slab, [own], here)
    parts = multiply_and_place(other, masked, mine)
    sent = lax.all_to_all(parts.reshape(n_row, here, nrows), "col", 0, 0)
    return sent.sum(0)


def solution(mesh):
    placed = (P(), P(), P("row", "col"), P("row", "col"))
    return jax.shard_map(
        body, mesh=mesh, in_specs=placed, out_specs=P("col", "row"), check_vma=False
    )
```

```python
import jax
import jax.numpy as jnp
from jax import lax
from jax.experimental import pallas as pl
from jax.experimental.pallas import tpu as pltpu
from jax.sharding import PartitionSpec as P

BAND = 128


def against(left, w):
    return lax.dot_general(left, w, (((1,), (1,)), ((), ())), preferred_element_type=jnp.float32)


def band_labels(start, band, occ_ref, vir):
    nocc, nvir = occ_ref.shape[0], vir.shape[1]
    row = start + lax.broadcasted_iota(jnp.int32, (band, 1), 0)
    chosen = lax.broadcasted_iota(jnp.int32, (band, nvir), 1) == row % nvir
    vir_part = jnp.sum(jnp.where(chosen, jnp.broadcast_to(vir, (band, nvir)), 0), axis=1, keepdims=True)
    first = start // nvir
    following = occ_ref[jnp.minimum(first + 1, nocc - 1)]
    return vir_part ^ jnp.where(row // nvir == first, occ_ref[first], following)


def mask_kernel(place_ref, occ_ref, vir_ref, *refs):
    *own_refs, w_ref, masked_ref, mine_ref, sems = refs
    nrows, width = masked_ref.shape
    nvir = vir_ref.shape[1]
    vir = vir_ref[...]
    spans = [pl.ds(start, BAND) for start in range(0, nrows, BAND)]
    copies = [pltpu.make_async_copy(w_ref.at[span], masked_ref.at[span], sems.at[i]) for i, span in enumerate(spans)]
    for copy in copies:
        copy.start()
    col_labels = [vir ^ occ_ref[place_ref[1] // nvir + part] for part in range(width // nvir)]

    def mask(i):
        row_labels = band_labels(place_ref[0] + i * BAND, BAND, occ_ref, vir)
        copies[i].wait()
        for part, labels in enumerate(col_labels):
            cols = pl.ds(part * nvir, nvir)
            w = masked_ref[spans[i], cols]
            masked_ref[spans[i], cols] = jnp.where(row_labels == labels, w, jnp.zeros_like(w))

    def multiply(i):
        for s, own_ref in enumerate(own_refs):
            product = against(own_ref[...], masked_ref[spans[i], :])
            mine_ref[s, :, :, spans[i]] = product.reshape(mine_ref.shape[1], mine_ref.shape[2], BAND)

    for i in range(len(spans)):
        mask(i)
        if i:
            multiply(i - 1)
    multiply(len(spans) - 1)


def mask_and_multiply(occ_irrep, vir_irrep, w_slab, own, here):
    nrows, width = w_slab.shape
    nvir = vir_irrep.shape[0]
    rows = own[0].shape[0]
    place = jnp.stack([lax.axis_index("row") * nrows, lax.axis_index("col") * width]).astype(jnp.int32)
    smem, vmem = pl.BlockSpec(memory_space=pltpu.SMEM), pl.BlockSpec(memory_space=pltpu.VMEM)
    return pl.pallas_call(
        mask_kernel,
        in_specs=[smem, smem, vmem] + [vmem] * len(own) + [pl.BlockSpec(memory_space=pltpu.HBM)],
        out_specs=[vmem, vmem],
        out_shape=[
            jax.ShapeDtypeStruct(w_slab.shape, w_slab.dtype),
            jax.ShapeDtypeStruct((len(own), rows // here, here, nrows), jnp.float32),
        ],
        scratch_shapes=[pltpu.SemaphoreType.DMA((nrows // BAND,))],
        compiler_params=pltpu.CompilerParams(vmem_limit_bytes=48 * 1024 * 1024),
        cost_estimate=pl.CostEstimate(
            flops=2 * len(own) * rows * width * nrows, bytes_accessed=4 * nrows * width, transcendentals=0
        ),
    )(place, occ_irrep, vir_irrep.reshape(1, nvir), *own, w_slab)


def place_kernel(me_ref, other_ref, w_ref, mine_ref, out_ref):
    core = me_ref[0] % 2
    planes = out_ref.shape[0]
    product = against(other_ref[...], w_ref[...]).reshape(mine_ref.shape)
    for value, at in ((mine_ref, core), (product, 1 - core)):
        for side in range(2):
            for p in range(planes):
                plane = p + at * (planes - 1 - 2 * p)
                out_ref[pl.ds(plane, 1), pl.ds(side ^ at, 1), pl.ds(at, 1)] = value[0, side * planes + p][None, None, None]


def multiply_and_place(other, masked, mine):
    nrows, width = masked.shape
    _, chips, here, _ = mine.shape
    shape = (chips // 2, 2, 2, here, nrows)
    me = lax.axis_index("row").astype(jnp.int32).reshape(1)
    vmem = pl.BlockSpec(memory_space=pltpu.VMEM)
    return pl.pallas_call(
        place_kernel,
        in_specs=[pl.BlockSpec(memory_space=pltpu.SMEM), vmem, vmem, vmem],
        out_specs=vmem,
        out_shape=jax.ShapeDtypeStruct(shape, jnp.float32),
        compiler_params=pltpu.CompilerParams(vmem_limit_bytes=8 * 1024 * 1024),
        cost_estimate=pl.CostEstimate(
            flops=2 * other.shape[0] * width * nrows, bytes_accessed=2 * nrows * width, transcendentals=0
        ),
    )(me, other, masked, mine)


def body(occ_irrep, vir_irrep, w_slab, amplitudes):
    nrows, width = w_slab.shape
    here = amplitudes.shape[0]
    n_row = lax.axis_size("row")
    chips = n_row // 2
    planes = chips // 2
    ways = [(0, 1, range(planes)), (1, 0, range(planes - 1, -1, -1))]
    cores = [[4 * p + 2 * side + core for side in ways[core][:2] for p in ways[core][2]] for core in range(2)]
    copies = jnp.broadcast_to(amplitudes[None], (chips, here, width))
    own = lax.all_to_all(copies, "row", 0, 0, axis_index_groups=cores).reshape(chips * here, width)
    other = lax.ppermute(own, "row", [(i, i ^ 1) for i in range(n_row)])
    masked, mine = mask_and_multiply(occ_irrep, vir_irrep, w_slab, [own], here)
    parts = multiply_and_place(other, masked, mine)
    sent = lax.all_to_all(parts.reshape(n_row, here, nrows), "col", 0, 0)
    return sent.sum(0)


def solution(mesh):
    placed = (P(), P(), P("row", "col"), P("row", "col"))
    return jax.shard_map(
        body, mesh=mesh, in_specs=placed, out_specs=P("col", "row"), check_vma=False
    )
```

```python
import jax
import jax.numpy as jnp
from jax import lax
from jax.experimental import pallas as pl
from jax.experimental.pallas import tpu as pltpu
from jax.sharding import PartitionSpec as P

BAND = 128


def against(left, w):
    return lax.dot_general(left, w, (((1,), (1,)), ((), ())), preferred_element_type=jnp.float32)


def band_labels(start, band, occ_ref, vir):
    nocc, nvir = occ_ref.shape[0], vir.shape[1]
    row = start + lax.broadcasted_iota(jnp.int32, (band, 1), 0)
    chosen = lax.broadcasted_iota(jnp.int32, (band, nvir), 1) == row % nvir
    vir_part = jnp.sum(jnp.where(chosen, jnp.broadcast_to(vir, (band, nvir)), 0), axis=1, keepdims=True)
    first = start // nvir
    following = occ_ref[jnp.minimum(first + 1, nocc - 1)]
    return vir_part ^ jnp.where(row // nvir == first, occ_ref[first], following)


def mask_kernel(place_ref, occ_ref, vir_ref, *refs):
    *own_refs, w_ref, masked_ref, mine_ref, sems = refs
    nrows, width = masked_ref.shape
    nvir = vir_ref.shape[1]
    vir = vir_ref[...]
    spans = [pl.ds(start, BAND) for start in range(0, nrows, BAND)]
    areas = [(i, part) for i in range(len(spans)) for part in range(width // nvir)]
    copies = {}
    for i, part in areas:
        area = (spans[i], pl.ds(part * nvir, nvir))
        copies[i, part] = pltpu.make_async_copy(w_ref.at[area], masked_ref.at[area], sems.at[i, part])
        copies[i, part].start()
    col_labels = [vir ^ occ_ref[place_ref[1] // nvir + part] for part in range(width // nvir)]

    def mask(i):
        row_labels = band_labels(place_ref[0] + i * BAND, BAND, occ_ref, vir)
        for part, labels in enumerate(col_labels):
            copies[i, part].wait()
            cols = pl.ds(part * nvir, nvir)
            w = masked_ref[spans[i], cols]
            masked_ref[spans[i], cols] = jnp.where(row_labels == labels, w, jnp.zeros_like(w))

    def multiply(i):
        for s, own_ref in enumerate(own_refs):
            product = against(own_ref[...], masked_ref[spans[i], :])
            mine_ref[s, :, :, spans[i]] = product.reshape(mine_ref.shape[1], mine_ref.shape[2], BAND)

    for i in range(len(spans)):
        mask(i)
        if i:
            multiply(i - 1)
    multiply(len(spans) - 1)


def mask_and_multiply(occ_irrep, vir_irrep, w_slab, own, here):
    nrows, width = w_slab.shape
    nvir = vir_irrep.shape[0]
    rows = own[0].shape[0]
    place = jnp.stack([lax.axis_index("row") * nrows, lax.axis_index("col") * width]).astype(jnp.int32)
    smem, vmem = pl.BlockSpec(memory_space=pltpu.SMEM), pl.BlockSpec(memory_space=pltpu.VMEM)
    return pl.pallas_call(
        mask_kernel,
        in_specs=[smem, smem, vmem] + [vmem] * len(own) + [pl.BlockSpec(memory_space=pltpu.HBM)],
        out_specs=[vmem, vmem],
        out_shape=[
            jax.ShapeDtypeStruct(w_slab.shape, w_slab.dtype),
            jax.ShapeDtypeStruct((len(own), rows // here, here, nrows), jnp.float32),
        ],
        scratch_shapes=[pltpu.SemaphoreType.DMA((nrows // BAND, width // nvir))],
        compiler_params=pltpu.CompilerParams(vmem_limit_bytes=48 * 1024 * 1024),
        cost_estimate=pl.CostEstimate(
            flops=2 * len(own) * rows * width * nrows, bytes_accessed=4 * nrows * width, transcendentals=0
        ),
    )(place, occ_irrep, vir_irrep.reshape(1, nvir), *own, w_slab)


def place_kernel(me_ref, other_ref, w_ref, mine_ref, out_ref):
    core = me_ref[0] % 2
    planes = out_ref.shape[0]
    product = against(other_ref[...], w_ref[...]).reshape(mine_ref.shape)
    for value, at in ((mine_ref, core), (product, 1 - core)):
        for side in range(2):
            for p in range(planes):
                plane = p + at * (planes - 1 - 2 * p)
                out_ref[pl.ds(plane, 1), pl.ds(side ^ at, 1), pl.ds(at, 1)] = value[0, side * planes + p][None, None, None]


def multiply_and_place(other, masked, mine):
    nrows, width = masked.shape
    _, chips, here, _ = mine.shape
    shape = (chips // 2, 2, 2, here, nrows)
    me = lax.axis_index("row").astype(jnp.int32).reshape(1)
    vmem = pl.BlockSpec(memory_space=pltpu.VMEM)
    return pl.pallas_call(
        place_kernel,
        in_specs=[pl.BlockSpec(memory_space=pltpu.SMEM), vmem, vmem, vmem],
        out_specs=vmem,
        out_shape=jax.ShapeDtypeStruct(shape, jnp.float32),
        compiler_params=pltpu.CompilerParams(vmem_limit_bytes=8 * 1024 * 1024),
        cost_estimate=pl.CostEstimate(
            flops=2 * other.shape[0] * width * nrows, bytes_accessed=2 * nrows * width, transcendentals=0
        ),
    )(me, other, masked, mine)


def body(occ_irrep, vir_irrep, w_slab, amplitudes):
    nrows, width = w_slab.shape
    here = amplitudes.shape[0]
    n_row = lax.axis_size("row")
    chips = n_row // 2
    planes = chips // 2
    ways = [(0, 1, range(planes)), (1, 0, range(planes - 1, -1, -1))]
    cores = [[4 * p + 2 * side + core for side in ways[core][:2] for p in ways[core][2]] for core in range(2)]
    copies = jnp.broadcast_to(amplitudes[None], (chips, here, width))
    own = lax.all_to_all(copies, "row", 0, 0, axis_index_groups=cores).reshape(chips * here, width)
    other = lax.ppermute(own, "row", [(i, i ^ 1) for i in range(n_row)])
    masked, mine = mask_and_multiply(occ_irrep, vir_irrep, w_slab, [own], here)
    parts = multiply_and_place(other, masked, mine)
    sent = lax.all_to_all(parts.reshape(n_row, here, nrows), "col", 0, 0)
    return sent.sum(0)


def solution(mesh):
    placed = (P(), P(), P("row", "col"), P("row", "col"))
    return jax.shard_map(
        body, mesh=mesh, in_specs=placed, out_specs=P("col", "row"), check_vma=False
    )
```
